32 devices in a mesh: chol: 4 (over y, x), pair: 8 (over z, core).
Axes of the slice: x: 2, y: 2, z: 4, core: 2. Of those that a mesh axis runs over, the one named last changes fastest.
Arguments:
- green: bfloat16 [2, 128, 147456], P(None, 'chol', 'pair'), may hold values from -6 to 6
- chol_rot: bfloat16 [147456, 1024], P('pair', 'chol'), may hold values from -0.015625 to 0.015625
Outputs:
- force_bias: float32 [2, 128, 1024], P(None, 'pair', 'chol')
The draws below stay inside these ranges and needn't reach their ends.
All inputs are finite; a program needn't handle non-finite values.
Results may differ from the reference program's by a relative error of at most 0.0003.
Values may be sent and summed in bfloat16 or wider, within the bound.
A program may use at most 64 MiB of HBM per device.

```python
import jax
import jax.numpy as jnp

PAIRS = 147456
NCHOL = 1024
WALKERS = 128


def strengthened(array, own_key, source, target, blocks, factor):
    def block_of(axis_at):
        return (jnp.arange(array.shape[axis_at]) // (array.shape[axis_at] // blocks)).reshape((-1,) + (1,) * (array.ndim - 1 - axis_at))

    first = jax.random.permutation(own_key, blocks)[block_of(target)]
    second = (block_of(target) + blocks // 2) % blocks
    return jnp.where((block_of(source) == first) | (block_of(source) == second), factor * array, array)


def level_of(own_key, dims, split, low, high):
    def one(axis_at, parts):
        heights = jax.random.uniform(jax.random.fold_in(jax.random.fold_in(own_key, 6), axis_at), (parts,), jnp.float32, low / len(split), high / len(split))
        return jnp.repeat(jnp.exp(heights), dims[axis_at] // parts).reshape((-1,) + (1,) * (len(dims) - axis_at - 1))

    loudness = one(*split[0])
    for cut in split[1:]:
        loudness = loudness * one(*cut)
    return loudness


def scatter_about(own_key, dims, deviation, reach, split=(), kind=jnp.bfloat16):
    values = jax.random.normal(own_key, dims, jnp.float32) * deviation
    if len(split) > 0:
        values = level_of(own_key, dims, split, -0.22, 0.18) * values
    return jnp.clip(values, min=-reach, max=reach).astype(kind)


def bell_draw_with(own_key, extent, scale, reach, cuts, heavy, held_as=jnp.bfloat16):
    entries = scale * jax.random.normal(own_key, extent, jnp.float32)
    if cuts:
        entries = entries * level_of(own_key, extent, cuts, -0.22, 0.18)
    return jnp.clip(strengthened(entries, jax.random.fold_in(own_key, 3), *heavy), -reach, reach).astype(held_as)


def setup_inputs(seed: int = 0) -> dict:
    streams_of = jax.random.split(jax.random.key(seed), 3)
    green = bell_draw_with(streams_of[0], (2, WALKERS, PAIRS), 1.0, 6.0, ((1, 4), (2, 8)), (2, 1, 8, 2.0))
    chol_rot = scatter_about(streams_of[1], (PAIRS, NCHOL), PAIRS ** -0.5, 0.015625, ((0, 8), (1, 4)))
    return dict(green=green, chol_rot=chol_rot)


def reference(green, chol_rot):
    real_bias = jnp.dot(green[0], chol_rot, preferred_element_type=jnp.float32)
    imag_bias = jnp.dot(green[1], chol_rot, preferred_element_type=jnp.float32)
    return jnp.stack([real_bias, imag_bias], axis=0)
```

```python
import functools

import jax
import jax.numpy as jnp
from jax import lax
from jax.experimental import pallas as pl
from jax.experimental.pallas import tpu as pltpu
from jax.sharding import PartitionSpec as P

MESH = pl.DeviceIdType.MESH
CHUNKS = 18
AHEAD = 4


def kernel(pairs, green, chol, out, near, far, weights, total, staged, arrived,
           own_sem, weight_sem, x_send, x_recv, y_send, y_recv, fx_send, fy_send, far_recv, sum_send, sum_recv):
    n, width = near.shape[0], near.shape[-1]
    half = n // 2
    share = out.shape[1]
    per_block = green.shape[1] // share
    i, j = lax.axis_index("chol"), lax.axis_index("pair")
    x, y = lax.rem(i, 2), i // 2
    across, along = i + 1 - 2 * x, i + 2 - 4 * y
    blocks = (i, across, along, 3 - i)

    barrier = pltpu.get_barrier_semaphore()
    for to in (across, along):
        pl.semaphore_signal(barrier, inc=1, device_id=(to, j), device_id_type=MESH)
    for step in range(1, pairs):
        pl.semaphore_signal(barrier, inc=1, device_id=(i, lax.rem(j + step, pairs)), device_id_type=MESH)

    def columns(c):
        return pl.ds(pl.multiple_of(c * width, width), width)

    def own(c):
        return pltpu.make_async_copy(green.at[:, :, columns(c)], near.at[c, 0], own_sem.at[c])

    def weight(c):
        return pltpu.make_async_copy(chol.at[columns(c), :], weights.at[c], weight_sem.at[c])

    def to_x(c):
        return pltpu.make_async_remote_copy(green.at[:, :, columns(c)], near.at[c, 1], x_send.at[c], x_recv.at[c],
                                            device_id=(across, j), device_id_type=MESH)

    def to_y(c):
        return pltpu.make_async_remote_copy(green.at[:, :, columns(c)], near.at[c, 2], y_send.at[c], y_recv.at[c],
                                            device_id=(along, j), device_id_type=MESH)

    def on_x(k):
        return pltpu.make_async_remote_copy(near.at[2 * k, 2], far.at[2 * k], fx_send.at[k], far_recv.at[2 * k],
                                            device_id=(across, j), device_id_type=MESH)

    def on_y(k):
        return pltpu.make_async_remote_copy(near.at[2 * k + 1, 1], far.at[2 * k + 1], fy_send.at[k],
                                            far_recv.at[2 * k + 1], device_id=(along, j), device_id_type=MESH)

    def loop(low, high, body):
        lax.fori_loop(low, high, lambda s, _: (body(s), 0)[1], 0)

    def start_local(c):
        own(c).start()
        weight(c).start()

    def start_own(c):
        to_x(c).start()
        to_y(c).start()

    def start_on(k):
        on_x(k).start()
        on_y(k).start()

    pl.semaphore_wait(barrier, pairs + 1)
    loop(0, AHEAD, start_own)
    loop(0, n, start_local)
    total[...] = jnp.zeros_like(total)

    def first(c):
        own(c).wait()
        weight(c).wait()
        rows = near[c].reshape(-1, width)
        total[: rows.shape[0]] += jnp.dot(rows, weights[c], preferred_element_type=jnp.float32)

    def arrive(c):
        to_x(c).wait_recv()
        to_y(c).wait_recv()

    def phase_a(s):
        arrive(s)
        start_own(s + AHEAD)
        first(s)

    def phase_b(s):
        arrive(s)
        start_on(s + AHEAD - n)
        first(s)

    loop(0, n - AHEAD, phase_a)
    loop(n - AHEAD, n, phase_b)

    block_rows = 2 * green.shape[1]

    def sum_copy(slot, h):
        to = blocks[slot] * per_block + h
        return to, pltpu.make_async_remote_copy(
            staged.at[slot, h], arrived.at[j], sum_send.at[slot, h], sum_recv.at[j],
            device_id=(i, to), device_id_type=MESH)

    def send_sums(slot):
        part = total[slot * block_rows : (slot + 1) * block_rows].reshape(2, green.shape[1], -1)
        for h in range(per_block):
            staged[slot, h] = part[:, h * share : (h + 1) * share]
            to, copy = sum_copy(slot, h)

            @pl.when(to != j)
            def _():
                copy.start()

            @pl.when(to == j)
            def _():
                arrived[j] = staged[slot, h]

    for slot in range(3):
        send_sums(slot)

    def last(k):
        on_x(k).wait_recv()
        on_y(k).wait_recv()

    def multiply_last(k):
        part = jnp.dot(far[2 * k].reshape(-1, width), weights[2 * k], preferred_element_type=jnp.float32)
        part += jnp.dot(far[2 * k + 1].reshape(-1, width), weights[2 * k + 1], preferred_element_type=jnp.float32)
        total[3 * block_rows :] += part

    def phase_c(k):
        last(k)
        start_on(k + AHEAD)
        multiply_last(k)

    def phase_d(k):
        last(k)
        multiply_last(k)

    loop(0, half - AHEAD, phase_c)
    loop(half - AHEAD, half, phase_d)
    send_sums(3)

    for slot in range(4):
        for h in range(per_block):
            to, copy = sum_copy(slot, h)

            @pl.when(to != j)
            def _():
                copy.wait_send()

    def end_own(c):
        to_x(c).wait_send()
        to_y(c).wait_send()

    def end_on(k):
        on_x(k).wait_send()
        on_y(k).wait_send()

    loop(0, n, end_own)
    loop(0, half, end_on)

    for source in range(pairs):
        @pl.when(source != j)
        def _():
            pltpu.make_async_remote_copy(staged.at[0, 0], arrived.at[source], sum_send.at[0, 0], sum_recv.at[source],
                                         device_id=(i, source), device_id_type=MESH).wait_recv()

    result = arrived[0]
    for source in range(1, pairs):
        result += arrived[source]
    out[...] = result


def local_kernel(pairs, green, chol_rot):
    parts, walkers, depth = green.shape
    columns = chol_rot.shape[1]
    n = CHUNKS
    width = depth // n
    share = 4 * walkers // pairs
    dma = pltpu.SemaphoreType.DMA
    return pl.pallas_call(
        functools.partial(kernel, pairs),
        out_shape=jax.ShapeDtypeStruct((parts, share, columns), jnp.float32),
        in_specs=[pl.BlockSpec(memory_space=pl.ANY)] * 2,
        out_specs=pl.BlockSpec(memory_space=pltpu.VMEM),
        scratch_shapes=[
            pltpu.VMEM((n, 3, parts, walkers, width), jnp.bfloat16),
            pltpu.VMEM((n, parts, walkers, width), jnp.bfloat16),
            pltpu.VMEM((n, width, columns), jnp.bfloat16),
            pltpu.VMEM((4 * parts * walkers, columns), jnp.float32),
            pltpu.VMEM((4, walkers // share, parts, share, columns), jnp.float32),
            pltpu.VMEM((pairs, parts, share, columns), jnp.float32),
            dma((n,)), dma((n,)), dma((n,)), dma((n,)), dma((n,)), dma((n,)),
            dma((n // 2,)), dma((n // 2,)), dma((n,)),
            dma((4, walkers // share)), dma((pairs,)),
        ],
        compiler_params=pltpu.CompilerParams(
            collective_id=0, has_side_effects=True, vmem_limit_bytes=56 * 1024 * 1024
        ),
        cost_estimate=pl.CostEstimate(
            flops=2 * 4 * parts * walkers * depth * columns,
            bytes_accessed=2 * depth * (columns + 3 * parts * walkers), transcendentals=0),
    )(green, chol_rot)


def local(green, chol_rot):
    partial_value = jnp.einsum(
        "cwp,pg->wcg",
        lax.all_gather(green, "chol", axis=1, tiled=True),
        chol_rot,
        preferred_element_type=jnp.float32,
    )
    summed = lax.psum_scatter(partial_value, "pair", scatter_dimension=0, tiled=True)
    return jnp.transpose(summed, (1, 0, 2))


def solution(mesh):
    chols, pairs = mesh.shape["chol"], mesh.shape["pair"]
    plane = chols == 4 and pairs % 4 == 0
    return jax.shard_map(
        functools.partial(local_kernel, pairs) if plane else local,
        mesh=mesh,
        in_specs=(P(None, "chol", "pair"), P("pair", "chol")),
        out_specs=P(None, "pair", "chol"),
        check_vma=False,
    )
```

```python
import functools

import jax
import jax.numpy as jnp
from jax import lax
from jax.experimental import pallas as pl
from jax.experimental.pallas import tpu as pltpu
from jax.sharding import PartitionSpec as P

MESH = pl.DeviceIdType.MESH
CHUNKS = 18
AHEAD = 4


def kernel(pairs, green, chol, out, near, far, weights, total, staged, arrived,
           own_sem, weight_sem, x_send, x_recv, y_send, y_recv, fx_send, fy_send, far_recv, sum_send, sum_recv, up, down):
    n, width = near.shape[0], near.shape[-1]
    half = n // 2
    share = out.shape[1]
    per_block = green.shape[1] // share
    i, j = lax.axis_index("chol"), lax.axis_index("pair")
    x, y = lax.rem(i, 2), i // 2
    across, along = i + 1 - 2 * x, i + 2 - 4 * y
    blocks = (i, across, along, 3 - i)

    barrier = pltpu.get_barrier_semaphore()
    for to in (across, along):
        pl.semaphore_signal(barrier, inc=1, device_id=(to, j), device_id_type=MESH)
    pl.semaphore_signal(barrier, inc=1, device_id=(i, j + 1 - 2 * lax.rem(j, 2)), device_id_type=MESH)
    has_below, has_above = j >= 2, j < pairs - 2

    @pl.when(has_below)
    def _():
        pl.semaphore_signal(barrier, inc=1, device_id=(i, j - 2), device_id_type=MESH)

    @pl.when(has_above)
    def _():
        pl.semaphore_signal(barrier, inc=1, device_id=(i, j + 2), device_id_type=MESH)

    def columns(c):
        return pl.ds(pl.multiple_of(c * width, width), width)

    def own(c):
        return pltpu.make_async_copy(green.at[:, :, columns(c)], near.at[c, 0], own_sem.at[c])

    def weight(c):
        return pltpu.make_async_copy(chol.at[columns(c), :], weights.at[c], weight_sem.at[c])

    def to_x(c):
        return pltpu.make_async_remote_copy(green.at[:, :, columns(c)], near.at[c, 1], x_send.at[c], x_recv.at[c],
                                            device_id=(across, j), device_id_type=MESH)

    def to_y(c):
        return pltpu.make_async_remote_copy(green.at[:, :, columns(c)], near.at[c, 2], y_send.at[c], y_recv.at[c],
                                            device_id=(along, j), device_id_type=MESH)

    def on_x(k):
        return pltpu.make_async_remote_copy(near.at[2 * k, 2], far.at[2 * k], fx_send.at[k], far_recv.at[2 * k],
                                            device_id=(across, j), device_id_type=MESH)

    def on_y(k):
        return pltpu.make_async_remote_copy(near.at[2 * k + 1, 1], far.at[2 * k + 1], fy_send.at[k],
                                            far_recv.at[2 * k + 1], device_id=(along, j), device_id_type=MESH)

    def loop(low, high, body):
        lax.fori_loop(low, high, lambda s, _: (body(s), 0)[1], 0)

    def start_local(c):
        own(c).start()
        weight(c).start()

    def start_own(c):
        to_x(c).start()
        to_y(c).start()

    def start_on(k):
        on_x(k).start()
        on_y(k).start()

    pl.semaphore_wait(barrier, 4 + (j + pairs - 2) // pairs - (j + 2) // pairs)
    loop(0, AHEAD, start_own)
    loop(0, n, start_local)
    total[...] = jnp.zeros_like(total)

    for has_from, has_to, to, token in ((has_below, has_above, j + 2, up), (has_above, has_below, j - 2, down)):
        @pl.when(has_from)
        def _():
            pl.semaphore_wait(token, 1)

        @pl.when(has_to)
        def _():
            pl.semaphore_signal(token, inc=1, device_id=(i, to), device_id_type=MESH)

    def first(c):
        own(c).wait()
        weight(c).wait()
        rows = near[c].reshape(-1, width)
        total[: rows.shape[0]] += jnp.dot(rows, weights[c], preferred_element_type=jnp.float32)

    def arrive(c):
        to_x(c).wait_recv()
        to_y(c).wait_recv()

    def phase_a(s):
        arrive(s)
        start_own(s + AHEAD)
        first(s)

    def phase_b(s):
        arrive(s)
        start_on(s + AHEAD - n)
        first(s)

    loop(0, n - AHEAD, phase_a)
    loop(n - AHEAD, n, phase_b)

    block_rows = 2 * green.shape[1]

    def sum_copy(slot, h):
        to = blocks[slot] * per_block + h
        return to, pltpu.make_async_remote_copy(
            staged.at[slot, h], arrived.at[j], sum_send.at[slot, h], sum_recv.at[j],
            device_id=(i, to), device_id_type=MESH)

    def send_sums(slot):
        part = total[slot * block_rows : (slot + 1) * block_rows].reshape(2, green.shape[1], -1)
        for h in range(per_block):
            staged[slot, h] = part[:, h * share : (h + 1) * share]
            to, copy = sum_copy(slot, h)

            @pl.when(to != j)
            def _():
                copy.start()

            @pl.when(to == j)
            def _():
                arrived[j] = staged[slot, h]

    for slot in range(3):
        send_sums(slot)

    def last(k):
        on_x(k).wait_recv()
        on_y(k).wait_recv()

    def multiply_last(k):
        part = jnp.dot(far[2 * k].reshape(-1, width), weights[2 * k], preferred_element_type=jnp.float32)
        part += jnp.dot(far[2 * k + 1].reshape(-1, width), weights[2 * k + 1], preferred_element_type=jnp.float32)
        total[3 * block_rows :] += part

    def phase_c(k):
        last(k)
        start_on(k + AHEAD)
        multiply_last(k)

    def phase_d(k):
        last(k)
        multiply_last(k)

    loop(0, half - AHEAD, phase_c)
    loop(half - AHEAD, half, phase_d)
    send_sums(3)

    for slot in range(4):
        for h in range(per_block):
            to, copy = sum_copy(slot, h)

            @pl.when(to != j)
            def _():
                copy.wait_send()

    def end_own(c):
        to_x(c).wait_send()
        to_y(c).wait_send()

    def end_on(k):
        on_x(k).wait_send()
        on_y(k).wait_send()

    loop(0, n, end_own)
    loop(0, half, end_on)

    for source in range(pairs):
        @pl.when(source != j)
        def _():
            pltpu.make_async_remote_copy(staged.at[0, 0], arrived.at[source], sum_send.at[0, 0], sum_recv.at[source],
                                         device_id=(i, source), device_id_type=MESH).wait_recv()

    result = arrived[0]
    for source in range(1, pairs):
        result += arrived[source]
    out[...] = result


def local_kernel(pairs, green, chol_rot):
    parts, walkers, depth = green.shape
    columns = chol_rot.shape[1]
    n = CHUNKS
    width = depth // n
    share = 4 * walkers // pairs
    dma = pltpu.SemaphoreType.DMA
    return pl.pallas_call(
        functools.partial(kernel, pairs),
        out_shape=jax.ShapeDtypeStruct((parts, share, columns), jnp.float32),
        in_specs=[pl.BlockSpec(memory_space=pl.ANY)] * 2,
        out_specs=pl.BlockSpec(memory_space=pltpu.VMEM),
        scratch_shapes=[
            pltpu.VMEM((n, 3, parts, walkers, width), jnp.bfloat16),
            pltpu.VMEM((n, parts, walkers, width), jnp.bfloat16),
            pltpu.VMEM((n, width, columns), jnp.bfloat16),
            pltpu.VMEM((4 * parts * walkers, columns), jnp.float32),
            pltpu.VMEM((4, walkers // share, parts, share, columns), jnp.float32),
            pltpu.VMEM((pairs, parts, share, columns), jnp.float32),
            dma((n,)), dma((n,)), dma((n,)), dma((n,)), dma((n,)), dma((n,)),
            dma((n // 2,)), dma((n // 2,)), dma((n,)),
            dma((4, walkers // share)), dma((pairs,)),
            pltpu.SemaphoreType.REGULAR, pltpu.SemaphoreType.REGULAR,
        ],
        compiler_params=pltpu.CompilerParams(
            collective_id=0, has_side_effects=True, vmem_limit_bytes=56 * 1024 * 1024
        ),
        cost_estimate=pl.CostEstimate(
            flops=2 * 4 * parts * walkers * depth * columns,
            bytes_accessed=2 * depth * (columns + 3 * parts * walkers), transcendentals=0),
    )(green, chol_rot)


def local(green, chol_rot):
    partial_value = jnp.einsum(
        "cwp,pg->wcg",
        lax.all_gather(green, "chol", axis=1, tiled=True),
        chol_rot,
        preferred_element_type=jnp.float32,
    )
    summed = lax.psum_scatter(partial_value, "pair", scatter_dimension=0, tiled=True)
    return jnp.transpose(summed, (1, 0, 2))


def solution(mesh):
    chols, pairs = mesh.shape["chol"], mesh.shape["pair"]
    plane = chols == 4 and pairs % 4 == 0
    return jax.shard_map(
        functools.partial(local_kernel, pairs) if plane else local,
        mesh=mesh,
        in_specs=(P(None, "chol", "pair"), P("pair", "chol")),
        out_specs=P(None, "pair", "chol"),
        check_vma=False,
    )
```

```python
import functools

import jax
import jax.numpy as jnp
from jax import lax
from jax.experimental import pallas as pl
from jax.experimental.pallas import tpu as pltpu
from jax.sharding import PartitionSpec as P

MESH = pl.DeviceIdType.MESH
CHUNKS = 12
AHEAD = 4


def kernel(pairs, green, chol, out, near, far, weights, total, staged, arrived,
           own_sem, weight_sem, x_send, x_recv, y_send, y_recv, fx_send, fy_send, far_recv, sum_send, sum_recv, up, down):
    n, width = near.shape[0], near.shape[-1]
    half = n // 2
    share = out.shape[1]
    per_block = green.shape[1] // share
    i, j = lax.axis_index("chol"), lax.axis_index("pair")
    x, y = lax.rem(i, 2), i // 2
    across, along = i + 1 - 2 * x, i + 2 - 4 * y
    blocks = (i, across, along, 3 - i)

    barrier = pltpu.get_barrier_semaphore()
    for to in (across, along):
        pl.semaphore_signal(barrier, inc=1, device_id=(to, j), device_id_type=MESH)
    pl.semaphore_signal(barrier, inc=1, device_id=(i, j + 1 - 2 * lax.rem(j, 2)), device_id_type=MESH)
    has_below, has_above = j >= 2, j < pairs - 2

    @pl.when(has_below)
    def _():
        pl.semaphore_signal(barrier, inc=1, device_id=(i, j - 2), device_id_type=MESH)

    @pl.when(has_above)
    def _():
        pl.semaphore_signal(barrier, inc=1, device_id=(i, j + 2), device_id_type=MESH)

    def columns(c):
        return pl.ds(pl.multiple_of(c * width, width), width)

    def own(c):
        return pltpu.make_async_copy(green.at[:, :, columns(c)], near.at[c, 0], own_sem)

    weight = pltpu.make_async_copy(chol, weights, weight_sem)

    def to_x(c):
        return pltpu.make_async_remote_copy(green.at[:, :, columns(c)], near.at[c, 1], x_send, x_recv.at[c],
                                            device_id=(across, j), device_id_type=MESH)

    def to_y(c):
        return pltpu.make_async_remote_copy(green.at[:, :, columns(c)], near.at[c, 2], y_send, y_recv.at[c],
                                            device_id=(along, j), device_id_type=MESH)

    def on_x(k):
        return pltpu.make_async_remote_copy(near.at[2 * k, 2], far.at[2 * k], fx_send, far_recv.at[2 * k],
                                            device_id=(across, j), device_id_type=MESH)

    def on_y(k):
        return pltpu.make_async_remote_copy(near.at[2 * k + 1, 1], far.at[2 * k + 1], fy_send,
                                            far_recv.at[2 * k + 1], device_id=(along, j), device_id_type=MESH)

    def loop(low, high, body):
        lax.fori_loop(low, high, lambda s, _: (body(s), 0)[1], 0)

    def start_local(c):
        own(c).start()

    def start_own(c):
        to_x(c).start()
        to_y(c).start()

    def start_on(k):
        on_x(k).start()
        on_y(k).start()

    pl.semaphore_wait(barrier, 4 + (j + pairs - 2) // pairs - (j + 2) // pairs)
    loop(0, AHEAD, start_own)
    weight.start()
    loop(0, n, start_local)
    total[...] = jnp.zeros_like(total)

    for has_from, has_to, to, token in ((has_below, has_above, j + 2, up), (has_above, has_below, j - 2, down)):
        @pl.when(has_from)
        def _():
            pl.semaphore_wait(token, 1)

        @pl.when(has_to)
        def _():
            pl.semaphore_signal(token, inc=1, device_id=(i, to), device_id_type=MESH)

    def first(c):
        rows = near[c].reshape(-1, width)
        total[: rows.shape[0]] += jnp.dot(rows, weights[c], preferred_element_type=jnp.float32)

    def arrive(c):
        to_x(c).wait_recv()
        to_y(c).wait_recv()

    def phase_a(s):
        arrive(s)
        start_own(s + AHEAD)
        first(s)

    def phase_b(s):
        arrive(s)
        start_on(s + AHEAD - n)
        first(s)

    pltpu.make_async_copy(near.at[:, 0], near.at[:, 0], own_sem).wait()
    weight.wait()
    loop(0, n - AHEAD, phase_a)
    loop(n - AHEAD, n, phase_b)

    block_rows = 2 * green.shape[1]

    def sum_copy(slot, h):
        to = blocks[slot] * per_block + h
        return to, pltpu.make_async_remote_copy(
            staged.at[slot, h], arrived.at[j], sum_send.at[slot, h], sum_recv.at[j],
            device_id=(i, to), device_id_type=MESH)

    def send_sums(slot):
        part = total[slot * block_rows : (slot + 1) * block_rows].reshape(2, green.shape[1], -1)
        for h in range(per_block):
            staged[slot, h] = part[:, h * share : (h + 1) * share]
            to, copy = sum_copy(slot, h)

            @pl.when(to != j)
            def _():
                copy.start()

            @pl.when(to == j)
            def _():
                arrived[j] = staged[slot, h]

    for slot in range(3):
        send_sums(slot)

    def end_sends(count, send):
        sent = near.at[pl.ds(0, count), 1]
        pltpu.make_async_remote_copy(sent, sent, send, x_recv.at[0], device_id=(across, j), device_id_type=MESH).wait_send()

    def last(k):
        on_x(k).wait_recv()
        on_y(k).wait_recv()

    def multiply_last(k):
        part = jnp.dot(far[2 * k].reshape(-1, width), weights[2 * k], preferred_element_type=jnp.float32)
        part += jnp.dot(far[2 * k + 1].reshape(-1, width), weights[2 * k + 1], preferred_element_type=jnp.float32)
        total[3 * block_rows :] += part

    def phase_c(k):
        last(k)
        start_on(k + AHEAD)
        multiply_last(k)

    def phase_d(k):
        last(k)
        multiply_last(k)

    loop(0, half - AHEAD, phase_c)
    end_sends(n, x_send)
    end_sends(n, y_send)
    loop(half - AHEAD, half, phase_d)
    send_sums(3)

    for slot in range(4):
        for h in range(per_block):
            to, copy = sum_copy(slot, h)

            @pl.when(to != j)
            def _():
                copy.wait_send()

    end_sends(half, fx_send)
    end_sends(half, fy_send)

    result = arrived[j]
    for step in range(1, pairs):
        source = lax.rem(j + step, pairs)
        pltpu.make_async_remote_copy(staged.at[0, 0], arrived.at[source], sum_send.at[0, 0], sum_recv.at[source],
                                     device_id=(i, source), device_id_type=MESH).wait_recv()
        result += arrived[source]
    out[...] = result


def local_kernel(pairs, green, chol_rot):
    parts, walkers, depth = green.shape
    columns = chol_rot.shape[1]
    n = CHUNKS
    width = depth // n
    share = 4 * walkers // pairs
    dma = pltpu.SemaphoreType.DMA
    return pl.pallas_call(
        functools.partial(kernel, pairs),
        out_shape=jax.ShapeDtypeStruct((parts, share, columns), jnp.float32),
        in_specs=[pl.BlockSpec(memory_space=pl.ANY)] * 2,
        out_specs=pl.BlockSpec(memory_space=pltpu.VMEM),
        scratch_shapes=[
            pltpu.VMEM((n, 3, parts, walkers, width), jnp.bfloat16),
            pltpu.VMEM((n, parts, walkers, width), jnp.bfloat16),
            pltpu.VMEM((n, width, columns), jnp.bfloat16),
            pltpu.VMEM((4 * parts * walkers, columns), jnp.float32),
            pltpu.VMEM((4, walkers // share, parts, share, columns), jnp.float32),
            pltpu.VMEM((pairs, parts, share, columns), jnp.float32),
            dma, dma, dma, dma((n,)), dma, dma((n,)), dma, dma, dma((n,)),
            dma((4, walkers // share)), dma((pairs,)),
            pltpu.SemaphoreType.REGULAR, pltpu.SemaphoreType.REGULAR,
        ],
        compiler_params=pltpu.CompilerParams(
            collective_id=0, has_side_effects=True, vmem_limit_bytes=56 * 1024 * 1024
        ),
        cost_estimate=pl.CostEstimate(
            flops=2 * 4 * parts * walkers * depth * columns,
            bytes_accessed=2 * depth * (columns + 3 * parts * walkers), transcendentals=0),
    )(green, chol_rot.reshape(n, width, columns))


def local(green, chol_rot):
    partial_value = jnp.einsum(
        "cwp,pg->wcg",
        lax.all_gather(green, "chol", axis=1, tiled=True),
        chol_rot,
        preferred_element_type=jnp.float32,
    )
    summed = lax.psum_scatter(partial_value, "pair", scatter_dimension=0, tiled=True)
    return jnp.transpose(summed, (1, 0, 2))


def solution(mesh):
    chols, pairs = mesh.shape["chol"], mesh.shape["pair"]
    plane = chols == 4 and pairs % 4 == 0
    return jax.shard_map(
        functools.partial(local_kernel, pairs) if plane else local,
        mesh=mesh,
        in_specs=(P(None, "chol", "pair"), P("pair", "chol")),
        out_specs=P(None, "pair", "chol"),
        check_vma=False,
    )
```

```python
import functools

import jax
import jax.numpy as jnp
from jax import lax
from jax.experimental import pallas as pl
from jax.experimental.pallas import tpu as pltpu
from jax.sharding import PartitionSpec as P

MESH = pl.DeviceIdType.MESH
CHUNKS = 12
AHEAD = 4


def kernel(pairs, green, chol, arrived, near, far, weights, total, staged,
           own_sem, weight_sem, x_send, x_recv, y_send, y_recv, fx_send, fy_send, far_recv, sum_send, sum_recv, keep_sem, up, down):
    n, width = near.shape[0], near.shape[-1]
    half = n // 2
    share = arrived.shape[2]
    per_block = green.shape[1] // share
    i, j = lax.axis_index("chol"), lax.axis_index("pair")
    x, y = lax.rem(i, 2), i // 2
    across, along = i + 1 - 2 * x, i + 2 - 4 * y
    blocks = (i, across, along, 3 - i)

    barrier = pltpu.get_barrier_semaphore()
    for to in (across, along):
        pl.semaphore_signal(barrier, inc=1, device_id=(to, j), device_id_type=MESH)
    pl.semaphore_signal(barrier, inc=1, device_id=(i, j + 1 - 2 * lax.rem(j, 2)), device_id_type=MESH)
    has_below, has_above = j >= 2, j < pairs - 2

    @pl.when(has_below)
    def _():
        pl.semaphore_signal(barrier, inc=1, device_id=(i, j - 2), device_id_type=MESH)

    @pl.when(has_above)
    def _():
        pl.semaphore_signal(barrier, inc=1, device_id=(i, j + 2), device_id_type=MESH)

    def columns(c):
        return pl.ds(pl.multiple_of(c * width, width), width)

    def own(c):
        return pltpu.make_async_copy(green.at[:, :, columns(c)], near.at[c, 0], own_sem)

    weight = pltpu.make_async_copy(chol, weights, weight_sem)

    def to_x(c):
        return pltpu.make_async_remote_copy(green.at[:, :, columns(c)], near.at[c, 1], x_send, x_recv.at[c],
                                            device_id=(across, j), device_id_type=MESH)

    def to_y(c):
        return pltpu.make_async_remote_copy(green.at[:, :, columns(c)], near.at[c, 2], y_send, y_recv.at[c],
                                            device_id=(along, j), device_id_type=MESH)

    def on_x(k):
        return pltpu.make_async_remote_copy(near.at[2 * k, 2], far.at[2 * k], fx_send, far_recv.at[2 * k],
                                            device_id=(across, j), device_id_type=MESH)

    def on_y(k):
        return pltpu.make_async_remote_copy(near.at[2 * k + 1, 1], far.at[2 * k + 1], fy_send,
                                            far_recv.at[2 * k + 1], device_id=(along, j), device_id_type=MESH)

    def loop(low, high, body):
        lax.fori_loop(low, high, lambda s, _: (body(s), 0)[1], 0)

    def start_local(c):
        own(c).start()

    def start_own(c):
        to_x(c).start()
        to_y(c).start()

    def start_on(k):
        on_x(k).start()
        on_y(k).start()

    pl.semaphore_wait(barrier, 4 + (j + pairs - 2) // pairs - (j + 2) // pairs)
    loop(0, AHEAD, start_own)
    weight.start()
    loop(0, n, start_local)
    total[...] = jnp.zeros_like(total)

    for has_from, has_to, to, token in ((has_below, has_above, j + 2, up), (has_above, has_below, j - 2, down)):
        @pl.when(has_from)
        def _():
            pl.semaphore_wait(token, 1)

        @pl.when(has_to)
        def _():
            pl.semaphore_signal(token, inc=1, device_id=(i, to), device_id_type=MESH)

    def first(c):
        rows = near[c].reshape(-1, width)
        total[: rows.shape[0]] += jnp.dot(rows, weights[c], preferred_element_type=jnp.float32)

    def arrive(c):
        to_x(c).wait_recv()
        to_y(c).wait_recv()

    def phase_a(s):
        arrive(s)
        start_own(s + AHEAD)
        first(s)

    def phase_b(s):
        arrive(s)
        start_on(s + AHEAD - n)
        first(s)

    pltpu.make_async_copy(near.at[:, 0], near.at[:, 0], own_sem).wait()
    weight.wait()
    loop(0, n - AHEAD, phase_a)
    loop(n - AHEAD, n, phase_b)

    block_rows = 2 * green.shape[1]

    def sum_copy(slot, h):
        to = blocks[slot] * per_block + h
        return to, pltpu.make_async_remote_copy(
            staged.at[slot, h], arrived.at[j], sum_send.at[slot, h], sum_recv.at[j],
            device_id=(i, to), device_id_type=MESH)

    def send_sums(slot):
        part = total[slot * block_rows : (slot + 1) * block_rows].reshape(2, green.shape[1], -1)
        for h in range(per_block):
            staged[slot, h] = part[:, h * share : (h + 1) * share]
            to, copy = sum_copy(slot, h)

            @pl.when(to != j)
            def _():
                copy.start()

            @pl.when(to == j)
            def _():
                pltpu.make_async_copy(staged.at[slot, h], arrived.at[j], keep_sem).start()

    for slot in range(3):
        send_sums(slot)

    def end_sends(count, send):
        sent = near.at[pl.ds(0, count), 1]
        pltpu.make_async_remote_copy(sent, sent, send, x_recv.at[0], device_id=(across, j), device_id_type=MESH).wait_send()

    def last(k):
        on_x(k).wait_recv()
        on_y(k).wait_recv()

    def multiply_last(k):
        part = jnp.dot(far[2 * k].reshape(-1, width), weights[2 * k], preferred_element_type=jnp.float32)
        part += jnp.dot(far[2 * k + 1].reshape(-1, width), weights[2 * k + 1], preferred_element_type=jnp.float32)
        total[3 * block_rows :] += part

    def phase_c(k):
        last(k)
        start_on(k + AHEAD)
        multiply_last(k)

    def phase_d(k):
        last(k)
        multiply_last(k)

    loop(0, half - AHEAD, phase_c)
    end_sends(n, x_send)
    end_sends(n, y_send)
    loop(half - AHEAD, half, phase_d)
    send_sums(3)

    for slot in range(4):
        for h in range(per_block):
            to, copy = sum_copy(slot, h)

            @pl.when(to != j)
            def _():
                copy.wait_send()

            @pl.when(to == j)
            def _():
                pltpu.make_async_copy(staged.at[slot, h], arrived.at[j], keep_sem).wait()

    end_sends(half, fx_send)
    end_sends(half, fy_send)

    for step in range(1, pairs):
        source = lax.rem(j + step, pairs)
        pltpu.make_async_remote_copy(staged.at[0, 0], arrived.at[source], sum_send.at[0, 0], sum_recv.at[source],
                                     device_id=(i, source), device_id_type=MESH).wait_recv()


def local_kernel(pairs, green, chol_rot):
    parts, walkers, depth = green.shape
    columns = chol_rot.shape[1]
    n = CHUNKS
    width = depth // n
    share = 4 * walkers // pairs
    dma = pltpu.SemaphoreType.DMA
    shares = pl.pallas_call(
        functools.partial(kernel, pairs),
        out_shape=jax.ShapeDtypeStruct((pairs, parts, share, columns), jnp.float32),
        in_specs=[pl.BlockSpec(memory_space=pl.ANY)] * 2,
        out_specs=pl.BlockSpec(memory_space=pl.ANY),
        scratch_shapes=[
            pltpu.VMEM((n, 3, parts, walkers, width), jnp.bfloat16),
            pltpu.VMEM((n, parts, walkers, width), jnp.bfloat16),
            pltpu.VMEM((n, width, columns), jnp.bfloat16),
            pltpu.VMEM((4 * parts * walkers, columns), jnp.float32),
            pltpu.VMEM((4, walkers // share, parts, share, columns), jnp.float32),
            dma, dma, dma, dma((n,)), dma, dma((n,)), dma, dma, dma((n,)),
            dma((4, walkers // share)), dma((pairs,)), dma,
            pltpu.SemaphoreType.REGULAR, pltpu.SemaphoreType.REGULAR,
        ],
        compiler_params=pltpu.CompilerParams(
            collective_id=0, has_side_effects=True, vmem_limit_bytes=56 * 1024 * 1024
        ),
        cost_estimate=pl.CostEstimate(
            flops=2 * 4 * parts * walkers * depth * columns,
            bytes_accessed=2 * depth * (columns + 3 * parts * walkers), transcendentals=0),
    )(green, chol_rot.reshape(n, width, columns))
    return jnp.sum(shares, axis=0)


def local(green, chol_rot):
    partial_value = jnp.einsum(
        "cwp,pg->wcg",
        lax.all_gather(green, "chol", axis=1, tiled=True),
        chol_rot,
        preferred_element_type=jnp.float32,
    )
    summed = lax.psum_scatter(partial_value, "pair", scatter_dimension=0, tiled=True)
    return jnp.transpose(summed, (1, 0, 2))


def solution(mesh):
    chols, pairs = mesh.shape["chol"], mesh.shape["pair"]
    plane = chols == 4 and pairs % 4 == 0
    return jax.shard_map(
        functools.partial(local_kernel, pairs) if plane else local,
        mesh=mesh,
        in_specs=(P(None, "chol", "pair"), P("pair", "chol")),
        out_specs=P(None, "pair", "chol"),
        check_vma=False,
    )
```

```python
import functools

import jax
import jax.numpy as jnp
from jax import lax
from jax.experimental import pallas as pl
from jax.experimental.pallas import tpu as pltpu
from jax.sharding import PartitionSpec as P

MESH = pl.DeviceIdType.MESH
CHUNKS = 8
AHEAD = 4


def kernel(pairs, green, chol, arrived, near, far, weights, total, staged,
           own_sem, weight_sem, x_send, x_recv, y_send, y_recv, fx_send, fy_send, far_recv, sum_send, sum_recv, keep_sem, up, down):
    n, width = near.shape[0], near.shape[-1]
    half = n // 2
    share = arrived.shape[2]
    per_block = green.shape[1] // share
    i, j = lax.axis_index("chol"), lax.axis_index("pair")
    x, y = lax.rem(i, 2), i // 2
    across, along = i + 1 - 2 * x, i + 2 - 4 * y
    blocks = (i, across, along, 3 - i)

    barrier = pltpu.get_barrier_semaphore()
    for to in (across, along):
        pl.semaphore_signal(barrier, inc=1, device_id=(to, j), device_id_type=MESH)
    pl.semaphore_signal(barrier, inc=1, device_id=(i, j + 1 - 2 * lax.rem(j, 2)), device_id_type=MESH)
    has_below, has_above = j >= 2, j < pairs - 2

    @pl.when(has_below)
    def _():
        pl.semaphore_signal(barrier, inc=1, device_id=(i, j - 2), device_id_type=MESH)

    @pl.when(has_above)
    def _():
        pl.semaphore_signal(barrier, inc=1, device_id=(i, j + 2), device_id_type=MESH)

    def columns(c):
        return pl.ds(pl.multiple_of(c * width, width), width)

    def own(c):
        return pltpu.make_async_copy(green.at[:, :, columns(c)], near.at[c, 0], own_sem)

    weight = pltpu.make_async_copy(chol, weights, weight_sem)

    def to_x(c):
        return pltpu.make_async_remote_copy(green.at[:, :, columns(c)], near.at[c, 1], x_send, x_recv.at[c],
                                            device_id=(across, j), device_id_type=MESH)

    def to_y(c):
        return pltpu.make_async_remote_copy(green.at[:, :, columns(c)], near.at[c, 2], y_send, y_recv.at[c],
                                            device_id=(along, j), device_id_type=MESH)

    def on_x(k):
        return pltpu.make_async_remote_copy(near.at[2 * k, 2], far.at[2 * k], fx_send, far_recv.at[2 * k],
                                            device_id=(across, j), device_id_type=MESH)

    def on_y(k):
        return pltpu.make_async_remote_copy(near.at[2 * k + 1, 1], far.at[2 * k + 1], fy_send,
                                            far_recv.at[2 * k + 1], device_id=(along, j), device_id_type=MESH)

    def loop(low, high, body):
        lax.fori_loop(low, high, lambda s, _: (body(s), 0)[1], 0)

    def start_local(c):
        own(c).start()

    def start_own(c):
        to_x(c).start()
        to_y(c).start()

    def start_on(k):
        on_x(k).start()
        on_y(k).start()

    pl.semaphore_wait(barrier, 4 + (j + pairs - 2) // pairs - (j + 2) // pairs)
    loop(0, AHEAD, start_own)
    weight.start()
    loop(0, n, start_local)
    total[...] = jnp.zeros_like(total)

    for has_from, has_to, to, token in ((has_below, has_above, j + 2, up), (has_above, has_below, j - 2, down)):
        @pl.when(has_from)
        def _():
            pl.semaphore_wait(token, 1)

        @pl.when(has_to)
        def _():
            pl.semaphore_signal(token, inc=1, device_id=(i, to), device_id_type=MESH)

    def first(c):
        rows = near[c].reshape(-1, width)
        total[: rows.shape[0]] += jnp.dot(rows, weights[c], preferred_element_type=jnp.float32)

    def arrive(c):
        to_x(c).wait_recv()
        to_y(c).wait_recv()

    def phase_a(s):
        arrive(s)
        start_own(s + AHEAD)
        first(s)

    def phase_b(s):
        arrive(s)
        start_on(s + AHEAD - n)
        first(s)

    pltpu.make_async_copy(near.at[:, 0], near.at[:, 0], own_sem).wait()
    weight.wait()
    loop(0, n - AHEAD, phase_a)
    loop(n - AHEAD, n, phase_b)

    block_rows = 2 * green.shape[1]

    def sum_copy(slot, h):
        to = blocks[slot] * per_block + h
        return to, pltpu.make_async_remote_copy(
            staged.at[slot, h], arrived.at[j], sum_send.at[slot, h], sum_recv.at[j],
            device_id=(i, to), device_id_type=MESH)

    def send_sums(slot):
        part = total[slot * block_rows : (slot + 1) * block_rows].reshape(2, green.shape[1], -1)
        for h in range(per_block):
            staged[slot, h] = part[:, h * share : (h + 1) * share]
            to, copy = sum_copy(slot, h)

            @pl.when(to != j)
            def _():
                copy.start()

            @pl.when(to == j)
            def _():
                pltpu.make_async_copy(staged.at[slot, h], arrived.at[j], keep_sem).start()

    for slot in range(3):
        send_sums(slot)

    def end_sends(count, send):
        sent = near.at[pl.ds(0, count), 1]
        pltpu.make_async_remote_copy(sent, sent, send, x_recv.at[0], device_id=(across, j), device_id_type=MESH).wait_send()

    def last(k):
        on_x(k).wait_recv()
        on_y(k).wait_recv()

    def multiply_last(k):
        part = jnp.dot(far[2 * k].reshape(-1, width), weights[2 * k], preferred_element_type=jnp.float32)
        part += jnp.dot(far[2 * k + 1].reshape(-1, width), weights[2 * k + 1], preferred_element_type=jnp.float32)
        total[3 * block_rows :] += part

    def phase_c(k):
        last(k)
        start_on(k + AHEAD)
        multiply_last(k)

    def phase_d(k):
        last(k)
        multiply_last(k)

    loop(0, half - AHEAD, phase_c)
    end_sends(n, x_send)
    end_sends(n, y_send)
    loop(half - AHEAD, half, phase_d)
    send_sums(3)

    for slot in range(4):
        for h in range(per_block):
            to, copy = sum_copy(slot, h)

            @pl.when(to != j)
            def _():
                copy.wait_send()

            @pl.when(to == j)
            def _():
                pltpu.make_async_copy(staged.at[slot, h], arrived.at[j], keep_sem).wait()

    end_sends(half, fx_send)
    end_sends(half, fy_send)

    for step in range(1, pairs):
        source = lax.rem(j + step, pairs)
        pltpu.make_async_remote_copy(staged.at[0, 0], arrived.at[source], sum_send.at[0, 0], sum_recv.at[source],
                                     device_id=(i, source), device_id_type=MESH).wait_recv()


def local_kernel(pairs, green, chol_rot):
    parts, walkers, depth = green.shape
    columns = chol_rot.shape[1]
    n = CHUNKS
    width = depth // n
    share = 4 * walkers // pairs
    dma = pltpu.SemaphoreType.DMA
    shares = pl.pallas_call(
        functools.partial(kernel, pairs),
        out_shape=jax.ShapeDtypeStruct((pairs, parts, share, columns), jnp.float32),
        in_specs=[pl.BlockSpec(memory_space=pl.ANY)] * 2,
        out_specs=pl.BlockSpec(memory_space=pl.ANY),
        scratch_shapes=[
            pltpu.VMEM((n, 3, parts, walkers, width), jnp.bfloat16),
            pltpu.VMEM((n, parts, walkers, width), jnp.bfloat16),
            pltpu.VMEM((n, width, columns), jnp.bfloat16),
            pltpu.VMEM((4 * parts * walkers, columns), jnp.float32),
            pltpu.VMEM((4, walkers // share, parts, share, columns), jnp.float32),
            dma, dma, dma, dma((n,)), dma, dma((n,)), dma, dma, dma((n,)),
            dma((4, walkers // share)), dma((pairs,)), dma,
            pltpu.SemaphoreType.REGULAR, pltpu.SemaphoreType.REGULAR,
        ],
        compiler_params=pltpu.CompilerParams(
            collective_id=0, has_side_effects=True, vmem_limit_bytes=56 * 1024 * 1024
        ),
        cost_estimate=pl.CostEstimate(
            flops=2 * 4 * parts * walkers * depth * columns,
            bytes_accessed=2 * depth * (columns + 3 * parts * walkers), transcendentals=0),
    )(green, chol_rot.reshape(n, width, columns))
    return jnp.sum(shares, axis=0)


def local(green, chol_rot):
    partial_value = jnp.einsum(
        "cwp,pg->wcg",
        lax.all_gather(green, "chol", axis=1, tiled=True),
        chol_rot,
        preferred_element_type=jnp.float32,
    )
    summed = lax.psum_scatter(partial_value, "pair", scatter_dimension=0, tiled=True)
    return jnp.transpose(summed, (1, 0, 2))


def solution(mesh):
    chols, pairs = mesh.shape["chol"], mesh.shape["pair"]
    plane = chols == 4 and pairs % 4 == 0
    return jax.shard_map(
        functools.partial(local_kernel, pairs) if plane else local,
        mesh=mesh,
        in_specs=(P(None, "chol", "pair"), P("pair", "chol")),
        out_specs=P(None, "pair", "chol"),
        check_vma=False,
    )
```
